32 devices in a mesh: tau: 2 (over y), wide: 8 (over z, x), narrow: 2 (over core).
Axes of the slice: x: 2, y: 2, z: 4, core: 2. Of those that a mesh axis runs over, the one named last changes fastest.
Arguments:
- integrals: bfloat16 [8, 32, 256, 512], P(None, 'narrow', 'wide'), may hold values from -0.5 to 0.5
- occupied: bfloat16 [4096, 768], P(('tau', 'wide')), parts along dimension 0, may hold values from -0.25 to 0.25
- virtual: bfloat16 [4096, 768], P(('tau', 'wide')), parts along dimension 0, may hold values from -0.25 to 0.25
- pattern: int32 [8, 2, 4], P('wide'), may hold values 0 or 1
Outputs:
- chi: float32 [512, 96], P(('tau', 'wide', 'narrow')), parts along dimension 0
The draws below stay inside these ranges and needn't reach their ends.
There are 2 independent parts, one for each index of `tau`. The reference program is written for one: setup_inputs(seed, part) draws one part's arguments, and reference() takes and returns one part's arrays. A program takes and returns all parts, laid end to end along the dimension named above; an argument that names none is the same for every part. Nothing has to cross between parts.
Inputs may be any that keep to these rules, and one draw needn't show every extreme that they name: `pattern`: 1 where a tile of the integrals is kept, 0 where screening drops it.
All inputs are finite; a program needn't handle non-finite values. No bound on the sum of `pattern` on one device may be relied on, other than what follows from the above.
Results may differ from the reference program's by a relative error of at most 0.0041.
Values may be sent and summed in bfloat16 or wider, within the bound.
A program may use at most 128 MiB of HBM per device.

```python
import jax
import jax.numpy as jnp
from jax import lax

BF_DEV = 256
REGIONS = 8
AUX_REG = 32
NBF = 2048
TPR = 2


def with_ends(drawn, own_key, low, high):
    longest = drawn.shape.index(max(drawn.shape))
    spots = []
    for shift in (0, 1):
        where = [jax.random.randint(jax.random.fold_in(own_key, axis), (), 0, length) for axis, length in enumerate(drawn.shape)]
        where[longest] = (where[longest] + shift) % drawn.shape[longest]
        spots.append(tuple(where))
    return drawn.at[spots[0]].set(low).at[spots[1]].set(high)


def block_levels(key, extent, cuts, smallest, high):
    gain = 1.0
    for dim, blocks in cuts:
        draws = jax.random.uniform(jax.random.fold_in(jax.random.fold_in(key, 6), dim), (blocks,), jnp.float32, smallest / len(cuts), high / len(cuts))
        gain = gain * jnp.repeat(jnp.exp(draws), extent[dim] // blocks).reshape((-1,) + (1,) * (len(extent) - 1 - dim))
    return gain


def scatter_about(own_key, extent, spread, bound, shards=(), kind=jnp.bfloat16):
    level = block_levels(own_key, extent, shards, -0.22, 0.18) if shards else 1.0
    result = jax.random.normal(own_key, extent, jnp.float32) * spread * level
    return jnp.minimum(jnp.maximum(result, -bound), bound).astype(kind)


def setup_inputs(seed: int = 0, part: int = 0) -> dict:
    splits = jax.random.split(jax.random.key(seed), 5)
    own_keys = jax.random.split(jax.random.fold_in(splits[4], part), 5)
    integrals = scatter_about(splits[0], (REGIONS, AUX_REG, BF_DEV, 2 * BF_DEV), 0.0625, 0.5, ((1, 2), (2, 8)))
    occupied = scatter_about(own_keys[1], (NBF, 3 * BF_DEV), (2 * BF_DEV) ** -0.5, 0.25, ((0, 8),))
    virtual = scatter_about(own_keys[2], (NBF, 3 * BF_DEV), (2 * BF_DEV) ** -0.5, 0.25, ((0, 8),))
    pattern = with_ends((jax.random.randint(splits[3], (REGIONS, TPR, 2 * TPR), 0, 3) < 2).astype(jnp.int32), jax.random.fold_in(splits[3], 1), 0, 1)
    return {"integrals": integrals, "occupied": occupied, "virtual": virtual, "pattern": pattern}


def screened(slab_block, pattern_rows):
    tiles_mu = pattern_rows.shape[0]
    tiles_nu = pattern_rows.shape[1]
    aux_count = slab_block.shape[0]
    tile_width = slab_block.shape[1] // tiles_mu
    shaped = slab_block.reshape(aux_count, tiles_mu, tile_width, tiles_nu, tile_width)
    keep_tile = pattern_rows.astype(slab_block.dtype)[None, :, None, :, None]
    return (shaped * keep_tile).reshape(slab_block.shape)


def windowed(slab_block, here_rows, next_rows):
    aux_count = slab_block.shape[0]
    basis_width = slab_block.shape[1]
    flattened = slab_block.reshape(aux_count * basis_width, 2 * basis_width)
    leading = jnp.dot(flattened[:, :basis_width], here_rows, preferred_element_type=jnp.float32)
    trailing = jnp.dot(flattened[:, basis_width:], next_rows[:, :2 * basis_width], preferred_element_type=jnp.float32)
    combined = leading + jnp.pad(trailing, ((0, 0), (basis_width, 0)))
    return combined.astype(jnp.bfloat16).reshape(aux_count, basis_width, 3 * basis_width)


def reference(integrals, occupied, virtual, pattern):
    def region_rows(green, region):
        return lax.dynamic_slice_in_dim(green, (region * BF_DEV).astype(jnp.int32), BF_DEV, 0)

    def images(region, green):
        slab_block = screened(lax.dynamic_index_in_dim(integrals, region, 0, keepdims=False),
                              lax.dynamic_index_in_dim(pattern, region, 0, keepdims=False))
        return windowed(slab_block, region_rows(green, region), region_rows(green, (region + 1) % REGIONS))

    def advance(state_pair, region):
        before, current = state_pair
        following = images((region + 1) % REGIONS, virtual)
        occ_image = images(region, occupied)
        pieces = (before, current, following)
        blocks = []
        for column in range(3):
            occ_part = occ_image[:, :, column * BF_DEV:(column + 1) * BF_DEV].astype(jnp.float32)
            virt_part = pieces[column][:, :, (2 - column) * BF_DEV:(3 - column) * BF_DEV].astype(jnp.float32)
            blocks.append(jnp.einsum("pml,qlm->pq", occ_part, virt_part, precision=lax.Precision.HIGHEST))
        return (current, following), jnp.concatenate(blocks, axis=1)

    initial = (images(jnp.int32(REGIONS - 1), virtual), images(jnp.int32(0), virtual))
    final_state, rows_out = lax.scan(advance, initial, jnp.arange(REGIONS, dtype=jnp.int32))
    return rows_out.reshape(REGIONS * AUX_REG, 3 * AUX_REG)
```

```python
import functools

import jax
import jax.numpy as jnp
from jax import lax
from jax.experimental import pallas as pl
from jax.experimental.pallas import tpu as pltpu
from jax.sharding import PartitionSpec as P


def passed_along(value, axis, steps):
    count = lax.axis_size(axis)
    pairs = [(source, (source + steps) % count) for source in range(count)]
    return lax.ppermute(value, axis, pairs)


def screened(slab_block, pattern_rows):
    tiles_mu = pattern_rows.shape[0]
    tiles_nu = pattern_rows.shape[1]
    aux_count = slab_block.shape[0]
    tile_width = slab_block.shape[1] // tiles_mu
    shaped = slab_block.reshape(aux_count, tiles_mu, tile_width, tiles_nu, tile_width)
    keep_tile = pattern_rows.astype(slab_block.dtype)[None, :, None, :, None]
    return (shaped * keep_tile).reshape(slab_block.shape)


def windowed(slab_block, here_rows, next_rows):
    aux_count = slab_block.shape[0]
    basis_width = slab_block.shape[1]
    flattened = slab_block.reshape(aux_count * basis_width, 2 * basis_width)
    leading = jnp.dot(flattened[:, :basis_width], here_rows, preferred_element_type=jnp.float32)
    trailing = jnp.dot(
        flattened[:, basis_width:],
        next_rows[:, : 2 * basis_width],
        preferred_element_type=jnp.float32,
    )
    combined = leading + jnp.pad(trailing, ((0, 0), (basis_width, 0)))
    return combined.astype(jnp.bfloat16).reshape(aux_count, basis_width, 3 * basis_width)


def plain_body(integrals, occupied, virtual, pattern):
    basis_width = occupied.shape[0]
    occ_next, virt_next = passed_along((occupied, virtual), "wide", -1)
    slab_block = screened(
        lax.all_to_all(integrals, "wide", split_axis=0, concat_axis=2, tiled=True)[0], pattern[0]
    )
    occ_image = windowed(slab_block, occupied, occ_next)
    virt_image = windowed(slab_block, virtual, virt_next)
    region_all = lax.all_gather(virt_image, "narrow", axis=0, tiled=True)
    received = [
        passed_along(
            region_all[:, :, (offset + 1) * basis_width : (offset + 2) * basis_width],
            "wide",
            offset,
        )
        for offset in (1, -1)
    ]
    paired = jnp.stack([received[0], region_all[:, :, basis_width : 2 * basis_width], received[1]])
    blocks = []
    for column in range(3):
        occ_part = occ_image[:, :, column * basis_width : (column + 1) * basis_width]
        blocks.append(
            lax.dot_general(
                occ_part,
                paired[column],
                (((1, 2), (2, 1)), ((), ())),
                preferred_element_type=jnp.float32,
            )
        )
    return jnp.concatenate(blocks, axis=1)


GROUPS = 2
NT = (((1,), (1,)), ((), ()))


def kernel(
    width, integrals, occupied, virtual, levels, chi,
    slab, slab_next, occ_rows, virt_rows, level_mine, level_next,
    virt_turned, keep, keep_next, occ_img, occ_img_next, virt_img, virt_img_next,
    sums, edge_out, edge_in,
    local_sem, first_send, first_recv, tau_send, tau_recv, core_send, core_recv,
    own_send, own_recv, green_send, green_recv, edge_send, edge_recv,
):
    t, k, n = (lax.axis_index(name) for name in ("tau", "wide", "narrow"))
    own_aux, rows, both = integrals.shape[1:]
    basis = both // 2
    part = own_aux // 2
    step = part // GROUPS
    other_tau = (1 - t, k, n)
    other_core = (t, k, 1 - n)
    behind = lax.rem(k + width - 1, width)
    ahead = lax.rem(k + 1, width)

    barrier = pltpu.get_barrier_semaphore()

    def greet(distance, carry):
        pl.semaphore_signal(barrier, inc=1, device_id=(t, lax.rem(k + distance, width), n))
        return carry

    lax.fori_loop(1, width, greet, 0)
    pl.semaphore_signal(barrier, inc=1, device_id=other_tau)
    pl.semaphore_signal(barrier, inc=1, device_id=other_core)
    pl.semaphore_wait(barrier, width + 1)

    def remote(source, target, send, recv, device):
        return pltpu.make_async_remote_copy(
            src_ref=source, dst_ref=target, send_sem=send, recv_sem=recv,
            device_id=device, device_id_type=pl.DeviceIdType.MESH,
        )

    def landing(kind, aux, count, source):
        buffer = (slab, slab_next)[kind]
        return buffer.at[pl.ds(aux, count), pl.ds(pl.multiple_of(source * rows, rows), rows), :]

    def stored(kind, aux, count, target):
        if kind == 0:
            return integrals.at[target, pl.ds(aux, count), :, :]
        return integrals.at[lax.rem(target + 1, width), pl.ds(aux, count), :, pl.ds(0, basis)]

    def first(kind, group, target, source):
        aux = part * t + step * group
        return remote(
            stored(kind, aux, step, target),
            landing(kind, own_aux * n + aux, step, source),
            first_send.at[kind, group, target], first_recv.at[kind, group, source],
            (t, target, n),
        )

    def over_tau(kind, group, source, half):
        block = landing(kind, own_aux * n + part * half + step * group, step, source)
        return remote(
            block, block, tau_send.at[kind, group, source], tau_recv.at[kind, group, source], other_tau
        )

    def over_core(kind, group, source, half, core):
        block = landing(kind, own_aux * core + part * half + step * group, step, source)
        which = jnp.where(half == t, 0, 1)
        return remote(
            block, block, core_send.at[kind, group, which, source],
            core_recv.at[kind, group, which, source], other_core,
        )

    def own_over_core(kind, core):
        return remote(
            stored(kind, 0, own_aux, k), landing(kind, own_aux * core, own_aux, k),
            own_send.at[kind], own_recv.at[kind], other_core,
        )

    def greens():
        return (
            remote(occupied.at[:, pl.ds(0, both)], occ_rows.at[pl.ds(basis, basis), :],
                   green_send.at[0], green_recv.at[0], (t, behind, n)),
            remote(virtual.at[:, pl.ds(0, both)], virt_rows.at[pl.ds(basis, basis), :],
                   green_send.at[1], green_recv.at[1], (t, behind, n)),
            remote(levels, level_next, green_send.at[2], green_recv.at[2], (t, behind, n)),
        )

    local = [
        pltpu.make_async_copy(occupied.at[:, pl.ds(basis, both)], occ_rows.at[pl.ds(0, basis), :], local_sem.at[0]),
        pltpu.make_async_copy(virtual.at[:, pl.ds(basis, both)], virt_rows.at[pl.ds(0, basis), :], local_sem.at[1]),
        pltpu.make_async_copy(levels, level_mine, local_sem.at[2]),
        pltpu.make_async_copy(stored(0, 0, own_aux, k), landing(0, own_aux * n, own_aux, k), local_sem.at[3]),
        pltpu.make_async_copy(stored(1, 0, own_aux, k), landing(1, own_aux * n, own_aux, k), local_sem.at[4]),
    ]

    def send_first(group):
        def at(distance, carry):
            target = lax.rem(k + distance, width)
            for kind in (0, 1):
                first(kind, group, target, k).start()
            return carry
        lax.fori_loop(1, width, at, 0)

    for copy in greens():
        copy.start()
    send_first(0)
    for copy in local:
        copy.start()
    for kind in (0, 1):
        own_over_core(kind, n).start()
    for group in range(1, GROUPS):
        send_first(group)

    for copy in local:
        copy.wait()
    for copy in greens():
        copy.wait_recv()

    tile = 128
    for target, level, columns in ((keep, level_mine, 4), (keep_next, level_next, 2)):
        for m in range(2):
            for j in range(columns):
                value = level[pl.ds(4 * m + j, 1), :]
                target[pl.ds(m * tile, tile), pl.ds(j * tile, tile)] = jnp.broadcast_to(
                    value, (tile, tile)).astype(jnp.bfloat16)
    virt_turned[...] = virt_rows[...].astype(jnp.float32).T.astype(jnp.bfloat16)

    def relay(group):
        def from_first(distance):
            source = lax.rem(k + width - distance, width)
            for kind in (0, 1):
                first(kind, group, source, source).wait_recv()
                over_tau(kind, group, source, t).start()
                over_core(kind, group, source, t, n).start()

        def from_tau(distance):
            source = lax.rem(k + width - distance, width)
            for kind in (0, 1):
                over_tau(kind, group, source, 1 - t).wait_recv()
                over_core(kind, group, source, 1 - t, n).start()

        def at(distance, carry):
            from_first(distance)
            from_tau(distance - 1)
            return carry

        from_first(1)
        lax.fori_loop(2, width, at, 0)
        from_tau(width - 1)

        def gathered(distance, carry):
            source = lax.rem(k + width - distance, width)
            for kind in (0, 1):
                over_core(kind, group, source, t, 1 - n).wait_recv()
                over_core(kind, group, source, 1 - t, 1 - n).wait_recv()
            return carry

        lax.fori_loop(1, width, gathered, 0)

    def images(group):
        def virt_at(step_index, carry):
            aux = (step_index // step) * part + step * group + step_index % step
            piece = slab[aux] * keep[...]
            virt_img[aux] = lax.dot_general(
                virt_turned[...], piece, NT, preferred_element_type=jnp.float32).astype(jnp.bfloat16)
            piece = slab_next[aux] * keep_next[...]
            virt_img_next[aux] = lax.dot_general(
                virt_turned[pl.ds(0, basis), pl.ds(basis, basis)], piece, NT,
                preferred_element_type=jnp.float32).astype(jnp.bfloat16)
            return carry

        lax.fori_loop(0, 4 * step, virt_at, 0)

        def occ_at(step_index, carry):
            mine = (step_index // step) * part + step * group + step_index % step
            aux = own_aux * n + mine
            occ_img[mine] = jnp.dot(
                slab[aux] * keep[...], occ_rows[...],
                preferred_element_type=jnp.float32).astype(jnp.bfloat16)
            occ_img_next[mine] = jnp.dot(
                slab_next[aux] * keep_next[...], occ_rows[pl.ds(basis, basis), pl.ds(0, basis)],
                preferred_element_type=jnp.float32).astype(jnp.bfloat16)
            return carry

        lax.fori_loop(0, 2 * step, occ_at, 0)

    for group in range(GROUPS):
        relay(group)
        if group == 0:
            for kind in (0, 1):
                own_over_core(kind, 1 - n).wait_recv()
        images(group)

    packed = 16
    all_aux = 2 * own_aux

    def paired(left, left_column, right, right_row):
        sums[...] = jnp.zeros_like(sums)

        def at(index, carry):
            start = pl.multiple_of(index * packed, packed)
            one = left[:, pl.ds(start, packed), pl.ds(left_column, basis)]
            two = right[:, pl.ds(right_row + start, packed), :]
            sums[...] += lax.dot_general(
                one.reshape(own_aux * packed, basis), two.reshape(all_aux * packed, basis), NT,
                preferred_element_type=jnp.float32)
            return carry

        lax.fori_loop(0, basis // packed, at, 0)
        shape = sums.shape
        equal = (lax.broadcasted_iota(jnp.int32, shape, 0) % packed
                 == lax.broadcasted_iota(jnp.int32, shape, 1) % packed)
        kept = jnp.where(equal, sums[...], 0.0).reshape(own_aux, packed, shape[1]).sum(axis=1)
        spread = (shape[1], 128)
        pick = (lax.broadcasted_iota(jnp.int32, spread, 0) // packed
                == lax.broadcasted_iota(jnp.int32, spread, 1)).astype(jnp.float32)
        return jnp.dot(kept, pick, precision=lax.Precision.HIGHEST, preferred_element_type=jnp.float32)

    edge_out[...] = paired(occ_img_next, 0, virt_img, basis)
    edge = remote(edge_out, edge_in, edge_send, edge_recv, (t, ahead, n))
    edge.start()
    same = paired(occ_img, 0, virt_img, 0)
    following = paired(occ_img, basis, virt_img_next, 0)
    edge.wait()
    chi[...] = jnp.concatenate(
        [edge_in[:, :all_aux], same[:, :all_aux], following[:, :all_aux]], axis=1)

    for group in range(GROUPS):
        def drained(distance, carry):
            other = lax.rem(k + distance, width)
            for kind in (0, 1):
                first(kind, group, other, k).wait_send()
                over_tau(kind, group, other, t).wait_send()
                over_core(kind, group, other, t, n).wait_send()
                over_core(kind, group, other, 1 - t, n).wait_send()
            return carry
        lax.fori_loop(1, width, drained, 0)
    for kind in (0, 1):
        own_over_core(kind, n).wait_send()
    for copy in greens():
        copy.wait_send()


def fused_body(width, integrals, occupied, virtual, pattern):
    own_aux, rows, both = integrals.shape[1:]
    basis = both // 2
    levels = jnp.broadcast_to(pattern.reshape(-1, 1).astype(jnp.float32), (pattern.size, 128))
    bf16, f32 = jnp.bfloat16, jnp.float32
    dma = pltpu.SemaphoreType.DMA
    grid = (2, GROUPS, width)
    anywhere = pl.BlockSpec(memory_space=pl.ANY)
    return pl.pallas_call(
        functools.partial(kernel, width),
        out_shape=jax.ShapeDtypeStruct((own_aux, 6 * own_aux), f32),
        in_specs=[anywhere] * 4,
        out_specs=pl.BlockSpec(memory_space=pltpu.VMEM),
        scratch_shapes=[
            pltpu.VMEM((2 * own_aux, basis, both), bf16),
            pltpu.VMEM((2 * own_aux, basis, basis), bf16),
            pltpu.VMEM((both, both), bf16),
            pltpu.VMEM((both, both), bf16),
            pltpu.VMEM(levels.shape, f32),
            pltpu.VMEM(levels.shape, f32),
            pltpu.VMEM((both, both), bf16),
            pltpu.VMEM((basis, both), bf16),
            pltpu.VMEM((basis, basis), bf16),
            pltpu.VMEM((own_aux, basis, both), bf16),
            pltpu.VMEM((own_aux, basis, basis), bf16),
            pltpu.VMEM((2 * own_aux, both, basis), bf16),
            pltpu.VMEM((2 * own_aux, basis, basis), bf16),
            pltpu.VMEM((16 * own_aux, 32 * own_aux), f32),
            pltpu.VMEM((own_aux, 128), f32),
            pltpu.VMEM((own_aux, 128), f32),
            dma((5,)), dma(grid), dma(grid), dma(grid), dma(grid),
            dma((2, GROUPS, 2, width)), dma((2, GROUPS, 2, width)),
            dma((2,)), dma((2,)), dma((3,)), dma((3,)), dma(()), dma(()),
        ],
        compiler_params=pltpu.CompilerParams(
            collective_id=0, has_side_effects=True, vmem_limit_bytes=56 * 2**20
        ),
    )(integrals, occupied, virtual, levels)


def body(sizes, integrals, occupied, virtual, pattern):
    if sizes["tau"] == 2 and sizes["narrow"] == 2 and integrals.shape[2] % 16 == 0:
        return fused_body(sizes["wide"], integrals, occupied, virtual, pattern)
    return plain_body(integrals, occupied, virtual, pattern)


def solution(mesh):
    in_specs = (
        P(None, "narrow", "wide", None),
        P(("tau", "wide"), None),
        P(("tau", "wide"), None),
        P("wide", None, None),
    )
    out_specs = P(("tau", "wide", "narrow"), None)
    return jax.shard_map(
        functools.partial(body, dict(mesh.shape)),
        mesh=mesh, in_specs=in_specs, out_specs=out_specs, check_vma=False,
    )
```

```python
import functools

import jax
import jax.numpy as jnp
from jax import lax
from jax.experimental import pallas as pl
from jax.experimental.pallas import tpu as pltpu
from jax.sharding import PartitionSpec as P


def passed_along(value, axis, steps):
    count = lax.axis_size(axis)
    pairs = [(source, (source + steps) % count) for source in range(count)]
    return lax.ppermute(value, axis, pairs)


def screened(slab_block, pattern_rows):
    tiles_mu = pattern_rows.shape[0]
    tiles_nu = pattern_rows.shape[1]
    aux_count = slab_block.shape[0]
    tile_width = slab_block.shape[1] // tiles_mu
    shaped = slab_block.reshape(aux_count, tiles_mu, tile_width, tiles_nu, tile_width)
    keep_tile = pattern_rows.astype(slab_block.dtype)[None, :, None, :, None]
    return (shaped * keep_tile).reshape(slab_block.shape)


def windowed(slab_block, here_rows, next_rows):
    aux_count = slab_block.shape[0]
    basis_width = slab_block.shape[1]
    flattened = slab_block.reshape(aux_count * basis_width, 2 * basis_width)
    leading = jnp.dot(flattened[:, :basis_width], here_rows, preferred_element_type=jnp.float32)
    trailing = jnp.dot(
        flattened[:, basis_width:],
        next_rows[:, : 2 * basis_width],
        preferred_element_type=jnp.float32,
    )
    combined = leading + jnp.pad(trailing, ((0, 0), (basis_width, 0)))
    return combined.astype(jnp.bfloat16).reshape(aux_count, basis_width, 3 * basis_width)


def plain_body(integrals, occupied, virtual, pattern):
    basis_width = occupied.shape[0]
    occ_next, virt_next = passed_along((occupied, virtual), "wide", -1)
    slab_block = screened(
        lax.all_to_all(integrals, "wide", split_axis=0, concat_axis=2, tiled=True)[0], pattern[0]
    )
    occ_image = windowed(slab_block, occupied, occ_next)
    virt_image = windowed(slab_block, virtual, virt_next)
    region_all = lax.all_gather(virt_image, "narrow", axis=0, tiled=True)
    received = [
        passed_along(
            region_all[:, :, (offset + 1) * basis_width : (offset + 2) * basis_width],
            "wide",
            offset,
        )
        for offset in (1, -1)
    ]
    paired = jnp.stack([received[0], region_all[:, :, basis_width : 2 * basis_width], received[1]])
    blocks = []
    for column in range(3):
        occ_part = occ_image[:, :, column * basis_width : (column + 1) * basis_width]
        blocks.append(
            lax.dot_general(
                occ_part,
                paired[column],
                (((1, 2), (2, 1)), ((), ())),
                preferred_element_type=jnp.float32,
            )
        )
    return jnp.concatenate(blocks, axis=1)


GROUPS = 2
LAG = 1
SPAN = 4
NT = (((1,), (1,)), ((), ()))


def kernel(
    width, integrals, occupied, virtual, levels, chi,
    slab, slab_next, occ_rows, virt_rows, level_mine, level_next,
    virt_turned, keep, keep_next, occ_img, occ_img_next, virt_img, virt_img_next,
    sums, edge_out, edge_in,
    local_sem, first_send, first_recv, tau_send, tau_recv, core_send, core_recv,
    own_send, own_recv, green_send, green_recv, edge_send, edge_recv, pair_send,
):
    t, k, n = (lax.axis_index(name) for name in ("tau", "wide", "narrow"))
    own_aux, rows, both = integrals.shape[1:]
    basis = both // 2
    part = own_aux // 2
    step = part // GROUPS
    other_tau = (1 - t, k, n)
    other_core = (t, k, 1 - n)
    behind = lax.rem(k + width - 1, width)
    ahead = lax.rem(k + 1, width)

    barrier = pltpu.get_barrier_semaphore()

    def greet(distance, carry):
        pl.semaphore_signal(barrier, inc=1, device_id=(t, lax.rem(k + distance, width), n))
        return carry

    lax.fori_loop(1, width, greet, 0)
    pl.semaphore_signal(barrier, inc=1, device_id=other_tau)
    pl.semaphore_signal(barrier, inc=1, device_id=other_core)
    pl.semaphore_wait(barrier, width + 1)

    def remote(source, target, send, recv, device):
        return pltpu.make_async_remote_copy(
            src_ref=source, dst_ref=target, send_sem=send, recv_sem=recv,
            device_id=device, device_id_type=pl.DeviceIdType.MESH,
        )

    def landing(kind, aux, count, source):
        buffer = (slab, slab_next)[kind]
        return buffer.at[pl.ds(aux, count), pl.ds(pl.multiple_of(source * rows, rows), rows), :]

    def stored(kind, aux, count, target):
        if kind == 0:
            return integrals.at[target, pl.ds(aux, count), :, :]
        return integrals.at[lax.rem(target + 1, width), pl.ds(aux, count), :, pl.ds(0, basis)]

    def first(kind, group, target, source):
        aux = part * t + step * group
        return remote(
            stored(kind, aux, step, target),
            landing(kind, own_aux * n + aux, step, source),
            first_send.at[kind, group, target], first_recv.at[kind, group, source],
            (t, target, n),
        )

    def over_tau(kind, group, source, half):
        block = landing(kind, own_aux * n + part * half + step * group, step, source)
        return remote(
            block, block, tau_send.at[kind, group, source], tau_recv.at[kind, group, source], other_tau
        )

    def over_core(kind, group, source, half, core):
        block = landing(kind, own_aux * core + part * half + step * group, step, source)
        which = jnp.where(half == t, 0, 1)
        return remote(
            block, block, core_send.at[kind, group, which, source],
            core_recv.at[kind, group, which, source], other_core,
        )

    def own_over_core(kind, core):
        return remote(
            stored(kind, 0, own_aux, k), landing(kind, own_aux * core, own_aux, k),
            own_send.at[kind], own_recv.at[kind], other_core,
        )

    def green_rows(core):
        return pl.ds(pl.multiple_of(core * (basis // 2), basis // 2), basis // 2)

    def green_landing(rows_ref, core):
        return rows_ref.at[pl.ds(pl.multiple_of(basis + core * (basis // 2), basis // 2), basis // 2), :]

    def greens():
        return [
            remote(green.at[green_rows(n), pl.ds(0, both)], green_landing(rows_ref, n),
                   green_send.at[i], green_recv.at[i], (t, behind, n))
            for i, (green, rows_ref) in enumerate(((occupied, occ_rows), (virtual, virt_rows)))
        ] + [remote(levels, level_next, green_send.at[2], green_recv.at[2], (t, behind, n))]

    def greens_over_core(core):
        return [
            remote(green_landing(rows_ref, core), green_landing(rows_ref, core),
                   green_send.at[3 + i], green_recv.at[3 + i], other_core)
            for i, rows_ref in enumerate((occ_rows, virt_rows))
        ]

    local = [
        pltpu.make_async_copy(occupied.at[:, pl.ds(basis, both)], occ_rows.at[pl.ds(0, basis), :], local_sem.at[0]),
        pltpu.make_async_copy(virtual.at[:, pl.ds(basis, both)], virt_rows.at[pl.ds(0, basis), :], local_sem.at[1]),
        pltpu.make_async_copy(levels, level_mine, local_sem.at[2]),
        pltpu.make_async_copy(stored(0, 0, own_aux, k), landing(0, own_aux * n, own_aux, k), local_sem.at[3]),
        pltpu.make_async_copy(stored(1, 0, own_aux, k), landing(1, own_aux * n, own_aux, k), local_sem.at[4]),
    ]

    def direct(target):
        return jnp.logical_or(target % 2 == 1, target == k - 1)

    def passes_on(source):
        return jnp.logical_and(k % 2 == 1, source != k - 1)

    def over_pair(group, source):
        aux = own_aux * n + part * t + step * group
        here = pl.ds(pl.multiple_of(source * rows, rows), rows)
        return remote(
            slab.at[pl.ds(aux, step), here, pl.ds(0, basis)], landing(1, aux, step, source),
            pair_send.at[group, source], first_recv.at[1, group, source], (t, behind, n),
        )

    def send_first(group):
        def at(distance, carry):
            target = lax.rem(k + distance, width)
            first(0, group, target, k).start()

            @pl.when(direct(target))
            def _():
                first(1, group, target, k).start()
            return carry
        lax.fori_loop(1, width, at, 0)

    for copy in greens():
        copy.start()
    send_first(0)
    for copy in local:
        copy.start()
    for kind in (0, 1):
        own_over_core(kind, n).start()
    for group in range(1, GROUPS):
        send_first(group)

    for copy in local:
        copy.wait()
    for copy in greens():
        copy.wait_recv()
    for copy in greens_over_core(n):
        copy.start()
    for copy in greens_over_core(1 - n):
        copy.wait_recv()

    tiles = levels.shape[0]
    tile = basis // tiles
    for target, level, columns in ((keep, level_mine, 2 * tiles), (keep_next, level_next, tiles)):
        for m in range(tiles):
            for j in range(columns):
                value = level[pl.ds(m, 1), pl.ds(j, 1)].astype(jnp.float32)
                target[pl.ds(m * tile, tile), pl.ds(j * tile, tile)] = jnp.broadcast_to(
                    value, (tile, tile)).astype(jnp.bfloat16)
    virt_turned[...] = virt_rows[...].astype(jnp.float32).T.astype(jnp.bfloat16)

    def from_first(group, distance):
        source = lax.rem(k + width - distance, width)
        for kind in (0, 1):
            first(kind, group, source, source).wait_recv()
            over_tau(kind, group, source, t).start()
            if kind == 0:
                @pl.when(passes_on(source))
                def _():
                    over_pair(group, source).start()
            over_core(kind, group, source, t, n).start()

    def from_tau(group, distance):
        source = lax.rem(k + width - distance, width)
        for kind in (0, 1):
            over_tau(kind, group, source, 1 - t).wait_recv()
            over_core(kind, group, source, 1 - t, n).start()

    def relay(group, low, high):
        def at(distance, carry):
            @pl.when(distance < width)
            def _():
                from_first(group, distance)

            @pl.when(distance > LAG)
            def _():
                from_tau(group, distance - LAG)
            return carry

        lax.fori_loop(low, high, at, 0)

    relay_steps = width - 1 + LAG

    def gathered(group):
        def at(distance, carry):
            source = lax.rem(k + width - distance, width)
            for kind in (0, 1):
                over_core(kind, group, source, t, 1 - n).wait_recv()
                over_core(kind, group, source, 1 - t, 1 - n).wait_recv()
            return carry

        lax.fori_loop(1, width, at, 0)

    def virt_images(aux, piece, piece_next):
        virt_img[aux] = lax.dot_general(
            virt_turned[...], piece, NT, preferred_element_type=jnp.float32).astype(jnp.bfloat16)
        virt_img_next[aux] = lax.dot_general(
            virt_turned[pl.ds(0, basis), pl.ds(basis, basis)], piece_next, NT,
            preferred_element_type=jnp.float32).astype(jnp.bfloat16)

    def images(group):
        turns = 2 * step

        def at(turn, carry):
            if group + 1 < GROUPS:
                relay(group + 1, 1 + turn * relay_steps // turns, 1 + (turn + 1) * relay_steps // turns)
            mine = (turn // step) * part + step * group + turn % step
            theirs = own_aux * (1 - n) + mine
            virt_images(theirs, slab[theirs] * keep[...], slab_next[theirs] * keep_next[...])
            aux = own_aux * n + mine
            piece = slab[aux] * keep[...]
            piece_next = slab_next[aux] * keep_next[...]
            virt_images(aux, piece, piece_next)
            occ_img[mine] = jnp.dot(
                piece, occ_rows[...], preferred_element_type=jnp.float32).astype(jnp.bfloat16)
            occ_img_next[mine] = jnp.dot(
                piece_next, occ_rows[pl.ds(basis, basis), pl.ds(0, basis)],
                preferred_element_type=jnp.float32).astype(jnp.bfloat16)
            return carry

        lax.fori_loop(0, turns, at, 0)

    relay(0, 1, relay_steps + 1)
    for kind in (0, 1):
        own_over_core(kind, 1 - n).wait_recv()
    for group in range(GROUPS):
        gathered(group)
        images(group)

    packed = 16
    all_aux = 2 * own_aux

    def paired(left, left_column, right, right_row):
        def at(index, total):
            start = pl.multiple_of(index * packed, packed)
            one = left[:, pl.ds(start, packed), pl.ds(left_column, basis)]
            two = right[:, pl.ds(right_row + start, packed), :]
            return total + lax.dot_general(
                two.reshape(all_aux * packed, basis), one.reshape(own_aux * packed, basis), NT,
                preferred_element_type=jnp.float32)

        sums[...] = jnp.zeros_like(sums)

        def several(index, carry):
            total = sums[...]
            for inner in range(SPAN):
                total = at(index * SPAN + inner, total)
            sums[...] = total
            return carry

        lax.fori_loop(0, basis // packed // SPAN, several, 0)
        shape = sums.shape
        equal = ((lax.broadcasted_iota(jnp.int32, shape, 0) ^ lax.broadcasted_iota(jnp.int32, shape, 1))
                 & (packed - 1)) == 0
        kept = jnp.where(equal, sums[...], 0.0).reshape(all_aux, packed, shape[1]).sum(axis=1)
        spread = (shape[1], own_aux)
        pick = ((lax.broadcasted_iota(jnp.int32, spread, 0) >> 4)
                == lax.broadcasted_iota(jnp.int32, spread, 1)).astype(jnp.float32)
        return lax.dot_general(
            pick, kept, (((0,), (1,)), ((), ())),
            precision=lax.Precision.HIGHEST, preferred_element_type=jnp.float32)

    edge_out[...] = paired(occ_img_next, 0, virt_img, basis)
    edge = remote(edge_out, edge_in, edge_send, edge_recv, (t, ahead, n))
    edge.start()
    same = paired(occ_img, 0, virt_img, 0)
    following = paired(occ_img, basis, virt_img_next, 0)
    edge.wait()
    chi[...] = jnp.concatenate(
        [edge_in[...], same, following], axis=1)

    for group in range(GROUPS):
        def drained(distance, carry):
            other = lax.rem(k + distance, width)
            first(0, group, other, k).wait_send()

            @pl.when(direct(other))
            def _():
                first(1, group, other, k).wait_send()

            @pl.when(passes_on(other))
            def _():
                over_pair(group, other).wait_send()

            for kind in (0, 1):
                over_tau(kind, group, other, t).wait_send()
                over_core(kind, group, other, t, n).wait_send()
                over_core(kind, group, other, 1 - t, n).wait_send()
            return carry
        lax.fori_loop(1, width, drained, 0)
    for kind in (0, 1):
        own_over_core(kind, n).wait_send()
    for copy in greens() + greens_over_core(n):
        copy.wait_send()


def fused_body(width, integrals, occupied, virtual, pattern):
    own_aux, rows, both = integrals.shape[1:]
    basis = both // 2
    levels = pattern[0]
    bf16, f32 = jnp.bfloat16, jnp.float32
    dma = pltpu.SemaphoreType.DMA
    grid = (2, GROUPS, width)
    anywhere = pl.BlockSpec(memory_space=pl.ANY)
    return pl.pallas_call(
        functools.partial(kernel, width),
        out_shape=jax.ShapeDtypeStruct((own_aux, 6 * own_aux), f32),
        in_specs=[anywhere] * 4,
        out_specs=pl.BlockSpec(memory_space=pltpu.VMEM),
        scratch_shapes=[
            pltpu.VMEM((2 * own_aux, basis, both), bf16),
            pltpu.VMEM((2 * own_aux, basis, basis), bf16),
            pltpu.VMEM((both, both), bf16),
            pltpu.VMEM((both, both), bf16),
            pltpu.VMEM(levels.shape, levels.dtype),
            pltpu.VMEM(levels.shape, levels.dtype),
            pltpu.VMEM((both, both), bf16),
            pltpu.VMEM((basis, both), bf16),
            pltpu.VMEM((basis, basis), bf16),
            pltpu.VMEM((own_aux, basis, both), bf16),
            pltpu.VMEM((own_aux, basis, basis), bf16),
            pltpu.VMEM((2 * own_aux, both, basis), bf16),
            pltpu.VMEM((2 * own_aux, basis, basis), bf16),
            pltpu.VMEM((32 * own_aux, 16 * own_aux), f32),
            pltpu.VMEM((own_aux, 2 * own_aux), f32),
            pltpu.VMEM((own_aux, 2 * own_aux), f32),
            dma((5,)), dma(grid), dma(grid), dma(grid), dma(grid),
            dma((2, GROUPS, 2, width)), dma((2, GROUPS, 2, width)),
            dma((2,)), dma((2,)), dma((5,)), dma((5,)), dma(()), dma(()), dma((GROUPS, width)),
        ],
        compiler_params=pltpu.CompilerParams(
            collective_id=0, has_side_effects=True, vmem_limit_bytes=56 * 2**20
        ),
    )(integrals, occupied, virtual, levels)


def body(sizes, integrals, occupied, virtual, pattern):
    if sizes["tau"] == 2 and sizes["narrow"] == 2 and integrals.shape[2] % 16 == 0 and sizes["wide"] % 2 == 0:
        return fused_body(sizes["wide"], integrals, occupied, virtual, pattern)
    return plain_body(integrals, occupied, virtual, pattern)


def solution(mesh):
    in_specs = (
        P(None, "narrow", "wide", None),
        P(("tau", "wide"), None),
        P(("tau", "wide"), None),
        P("wide", None, None),
    )
    out_specs = P(("tau", "wide", "narrow"), None)
    return jax.shard_map(
        functools.partial(body, dict(mesh.shape)),
        mesh=mesh, in_specs=in_specs, out_specs=out_specs, check_vma=False,
    )
```

```python
import functools

import jax
import jax.numpy as jnp
from jax import lax
from jax.experimental import pallas as pl
from jax.experimental.pallas import tpu as pltpu
from jax.sharding import PartitionSpec as P


def passed_along(value, axis, steps):
    count = lax.axis_size(axis)
    pairs = [(source, (source + steps) % count) for source in range(count)]
    return lax.ppermute(value, axis, pairs)


def screened(slab_block, pattern_rows):
    tiles_mu = pattern_rows.shape[0]
    tiles_nu = pattern_rows.shape[1]
    aux_count = slab_block.shape[0]
    tile_width = slab_block.shape[1] // tiles_mu
    shaped = slab_block.reshape(aux_count, tiles_mu, tile_width, tiles_nu, tile_width)
    keep_tile = pattern_rows.astype(slab_block.dtype)[None, :, None, :, None]
    return (shaped * keep_tile).reshape(slab_block.shape)


def windowed(slab_block, here_rows, next_rows):
    aux_count = slab_block.shape[0]
    basis_width = slab_block.shape[1]
    flattened = slab_block.reshape(aux_count * basis_width, 2 * basis_width)
    leading = jnp.dot(flattened[:, :basis_width], here_rows, preferred_element_type=jnp.float32)
    trailing = jnp.dot(
        flattened[:, basis_width:],
        next_rows[:, : 2 * basis_width],
        preferred_element_type=jnp.float32,
    )
    combined = leading + jnp.pad(trailing, ((0, 0), (basis_width, 0)))
    return combined.astype(jnp.bfloat16).reshape(aux_count, basis_width, 3 * basis_width)


def plain_body(integrals, occupied, virtual, pattern):
    basis_width = occupied.shape[0]
    occ_next, virt_next = passed_along((occupied, virtual), "wide", -1)
    slab_block = screened(
        lax.all_to_all(integrals, "wide", split_axis=0, concat_axis=2, tiled=True)[0], pattern[0]
    )
    occ_image = windowed(slab_block, occupied, occ_next)
    virt_image = windowed(slab_block, virtual, virt_next)
    region_all = lax.all_gather(virt_image, "narrow", axis=0, tiled=True)
    received = [
        passed_along(
            region_all[:, :, (offset + 1) * basis_width : (offset + 2) * basis_width],
            "wide",
            offset,
        )
        for offset in (1, -1)
    ]
    paired = jnp.stack([received[0], region_all[:, :, basis_width : 2 * basis_width], received[1]])
    blocks = []
    for column in range(3):
        occ_part = occ_image[:, :, column * basis_width : (column + 1) * basis_width]
        blocks.append(
            lax.dot_general(
                occ_part,
                paired[column],
                (((1, 2), (2, 1)), ((), ())),
                preferred_element_type=jnp.float32,
            )
        )
    return jnp.concatenate(blocks, axis=1)


GROUPS = 2
LAG = 2
SPAN = 16
NT = (((1,), (1,)), ((), ()))


def kernel(
    width, integrals, occupied, virtual, levels, chi,
    slab, slab_next, occ_rows, virt_rows, level_mine, level_next,
    virt_turned, keep, keep_next, occ_img, occ_img_next, virt_img, virt_img_next,
    sums, edge_out, edge_in,
    local_sem, first_send, first_recv, tau_send, tau_recv, core_send, core_recv,
    own_send, own_recv, green_send, green_recv, edge_send, edge_recv, pair_send,
):
    t, k, n = (lax.axis_index(name) for name in ("tau", "wide", "narrow"))
    own_aux, rows, both = integrals.shape[1:]
    basis = both // 2
    part = own_aux // 2
    step = part // GROUPS
    other_tau = (1 - t, k, n)
    other_core = (t, k, 1 - n)
    behind = lax.rem(k + width - 1, width)
    ahead = lax.rem(k + 1, width)

    barrier = pltpu.get_barrier_semaphore()

    def greet(distance, carry):
        pl.semaphore_signal(barrier, inc=1, device_id=(t, lax.rem(k + distance, width), n))
        return carry

    lax.fori_loop(1, width, greet, 0)
    pl.semaphore_signal(barrier, inc=1, device_id=other_tau)
    pl.semaphore_signal(barrier, inc=1, device_id=other_core)
    pl.semaphore_wait(barrier, width + 1)

    def remote(source, target, send, recv, device):
        return pltpu.make_async_remote_copy(
            src_ref=source, dst_ref=target, send_sem=send, recv_sem=recv,
            device_id=device, device_id_type=pl.DeviceIdType.MESH,
        )

    def landing(kind, aux, count, source):
        buffer = (slab, slab_next)[kind]
        return buffer.at[pl.ds(aux, count), pl.ds(pl.multiple_of(source * rows, rows), rows), :]

    def stored(kind, aux, count, target):
        if kind == 0:
            return integrals.at[target, pl.ds(aux, count), :, :]
        return integrals.at[lax.rem(target + 1, width), pl.ds(aux, count), :, pl.ds(0, basis)]

    def first(kind, group, target, source):
        aux = part * t + step * group
        return remote(
            stored(kind, aux, step, target),
            landing(kind, own_aux * n + aux, step, source),
            first_send.at[kind, group, target], first_recv.at[kind, group, source],
            (t, target, n),
        )

    def over_tau(kind, group, source, half):
        block = landing(kind, own_aux * n + part * half + step * group, step, source)
        return remote(
            block, block, tau_send.at[kind, group, source], tau_recv.at[kind, group, source], other_tau
        )

    def over_core(kind, group, source, half, core):
        block = landing(kind, own_aux * core + part * half + step * group, step, source)
        which = jnp.where(half == t, 0, 1)
        return remote(
            block, block, core_send.at[kind, group, which, source],
            core_recv.at[kind, group, which, source], other_core,
        )

    def own_over_core(kind, core):
        return remote(
            stored(kind, 0, own_aux, k), landing(kind, own_aux * core, own_aux, k),
            own_send.at[kind], own_recv.at[kind], other_core,
        )

    def green_rows(core):
        return pl.ds(pl.multiple_of(core * (basis // 2), basis // 2), basis // 2)

    def green_landing(rows_ref, core):
        return rows_ref.at[pl.ds(pl.multiple_of(basis + core * (basis // 2), basis // 2), basis // 2), :]

    def greens():
        return [
            remote(green.at[green_rows(n), pl.ds(0, both)], green_landing(rows_ref, n),
                   green_send.at[i], green_recv.at[i], (t, behind, n))
            for i, (green, rows_ref) in enumerate(((occupied, occ_rows), (virtual, virt_rows)))
        ] + [remote(levels, level_next, green_send.at[2], green_recv.at[2], (t, behind, n))]

    def greens_over_core(core):
        return [
            remote(green_landing(rows_ref, core), green_landing(rows_ref, core),
                   green_send.at[3 + i], green_recv.at[3 + i], other_core)
            for i, rows_ref in enumerate((occ_rows, virt_rows))
        ]

    local = [
        pltpu.make_async_copy(occupied.at[:, pl.ds(basis, both)], occ_rows.at[pl.ds(0, basis), :], local_sem.at[0]),
        pltpu.make_async_copy(virtual.at[:, pl.ds(basis, both)], virt_rows.at[pl.ds(0, basis), :], local_sem.at[1]),
        pltpu.make_async_copy(levels, level_mine, local_sem.at[2]),
        pltpu.make_async_copy(stored(0, 0, own_aux, k), landing(0, own_aux * n, own_aux, k), local_sem.at[3]),
        pltpu.make_async_copy(stored(1, 0, own_aux, k), landing(1, own_aux * n, own_aux, k), local_sem.at[4]),
    ]

    def direct(target):
        return jnp.logical_or(target % 2 == 1, target == k - 1)

    def passes_on(source):
        return jnp.logical_and(k % 2 == 1, source != k - 1)

    def over_pair(group, source):
        aux = own_aux * n + part * t + step * group
        here = pl.ds(pl.multiple_of(source * rows, rows), rows)
        return remote(
            slab.at[pl.ds(aux, step), here, pl.ds(0, basis)], landing(1, aux, step, source),
            pair_send.at[group, source], first_recv.at[1, group, source], (t, behind, n),
        )

    def send_first(group):
        def at(distance, carry):
            target = lax.rem(k + distance, width)
            first(0, group, target, k).start()

            @pl.when(direct(target))
            def _():
                first(1, group, target, k).start()
            return carry
        lax.fori_loop(1, width, at, 0)

    for copy in greens():
        copy.start()
    send_first(0)
    for copy in local:
        copy.start()
    for kind in (0, 1):
        own_over_core(kind, n).start()
    for group in range(1, GROUPS):
        send_first(group)

    for copy in local:
        copy.wait()
    for copy in greens():
        copy.wait_recv()
    for copy in greens_over_core(n):
        copy.start()
    for copy in greens_over_core(1 - n):
        copy.wait_recv()

    tiles = levels.shape[0]
    tile = basis // tiles
    for target, level, columns in ((keep, level_mine, 2 * tiles), (keep_next, level_next, tiles)):
        for m in range(tiles):
            for j in range(columns):
                value = level[pl.ds(m, 1), pl.ds(j, 1)].astype(jnp.float32)
                target[pl.ds(m * tile, tile), pl.ds(j * tile, tile)] = jnp.broadcast_to(
                    value, (tile, tile)).astype(jnp.bfloat16)
    virt_turned[...] = virt_rows[...].astype(jnp.float32).T.astype(jnp.bfloat16)

    def from_first(group, distance):
        source = lax.rem(k + width - distance, width)
        for kind in (0, 1):
            first(kind, group, source, source).wait_recv()
            over_tau(kind, group, source, t).start()
            if kind == 0:
                @pl.when(passes_on(source))
                def _():
                    over_pair(group, source).start()
            over_core(kind, group, source, t, n).start()

    def from_tau(group, distance):
        source = lax.rem(k + width - distance, width)
        for kind in (0, 1):
            over_tau(kind, group, source, 1 - t).wait_recv()
            over_core(kind, group, source, 1 - t, n).start()

    def relay(group, low, high):
        def at(distance, carry):
            @pl.when(distance < width)
            def _():
                from_first(group, distance)

            @pl.when(distance > LAG)
            def _():
                from_tau(group, distance - LAG)
            return carry

        lax.fori_loop(low, high, at, 0)

    relay_steps = width - 1 + LAG

    def gathered(group):
        def at(distance, carry):
            source = lax.rem(k + width - distance, width)
            for kind in (0, 1):
                over_core(kind, group, source, t, 1 - n).wait_recv()
                over_core(kind, group, source, 1 - t, 1 - n).wait_recv()
            return carry

        lax.fori_loop(1, width, at, 0)

    def virt_images(aux, piece, piece_next):
        virt_img[aux] = lax.dot_general(
            virt_turned[...], piece, NT, preferred_element_type=jnp.float32).astype(jnp.bfloat16)
        virt_img_next[aux] = lax.dot_general(
            virt_turned[pl.ds(0, basis), pl.ds(basis, basis)], piece_next, NT,
            preferred_element_type=jnp.float32).astype(jnp.bfloat16)

    def images(group):
        turns = 2 * step

        def at(turn, carry):
            if group + 1 < GROUPS:
                relay(group + 1, 1 + turn * relay_steps // turns, 1 + (turn + 1) * relay_steps // turns)
            mine = (turn // step) * part + step * group + turn % step
            theirs = own_aux * (1 - n) + mine
            virt_images(theirs, slab[theirs] * keep[...], slab_next[theirs] * keep_next[...])
            aux = own_aux * n + mine
            piece = slab[aux] * keep[...]
            piece_next = slab_next[aux] * keep_next[...]
            virt_images(aux, piece, piece_next)
            occ_img[mine] = jnp.dot(
                piece, occ_rows[...], preferred_element_type=jnp.float32).astype(jnp.bfloat16)
            occ_img_next[mine] = jnp.dot(
                piece_next, occ_rows[pl.ds(basis, basis), pl.ds(0, basis)],
                preferred_element_type=jnp.float32).astype(jnp.bfloat16)
            return carry

        lax.fori_loop(0, turns, at, 0)

    relay(0, 1, relay_steps + 1)
    for kind in (0, 1):
        own_over_core(kind, 1 - n).wait_recv()
    for group in range(GROUPS):
        gathered(group)
        images(group)

    packed = 16
    all_aux = 2 * own_aux

    def paired(left, left_column, right, right_row):
        def at(index, total):
            start = pl.multiple_of(index * packed, packed)
            one = left[:, pl.ds(start, packed), pl.ds(left_column, basis)]
            two = right[:, pl.ds(right_row + start, packed), :]
            return total + lax.dot_general(
                two.reshape(all_aux * packed, basis), one.reshape(own_aux * packed, basis), NT,
                preferred_element_type=jnp.float32)

        sums[...] = jnp.zeros_like(sums)

        def several(index, carry):
            total = sums[...]
            for inner in range(SPAN):
                total = at(index * SPAN + inner, total)
            sums[...] = total
            return carry

        lax.fori_loop(0, basis // packed // SPAN, several, 0)
        shape = sums.shape
        equal = ((lax.broadcasted_iota(jnp.int32, shape, 0) ^ lax.broadcasted_iota(jnp.int32, shape, 1))
                 & (packed - 1)) == 0
        kept = jnp.where(equal, sums[...], 0.0).reshape(all_aux, packed, shape[1]).sum(axis=1)
        spread = (shape[1], own_aux)
        pick = ((lax.broadcasted_iota(jnp.int32, spread, 0) >> 4)
                == lax.broadcasted_iota(jnp.int32, spread, 1)).astype(jnp.float32)
        return lax.dot_general(
            pick, kept, (((0,), (1,)), ((), ())),
            precision=lax.Precision.HIGHEST, preferred_element_type=jnp.float32)

    edge_out[...] = paired(occ_img_next, 0, virt_img, basis)
    edge = remote(edge_out, edge_in, edge_send, edge_recv, (t, ahead, n))
    edge.start()
    same = paired(occ_img, 0, virt_img, 0)
    following = paired(occ_img, basis, virt_img_next, 0)
    edge.wait()
    chi[...] = jnp.concatenate(
        [edge_in[...], same, following], axis=1)

    for group in range(GROUPS):
        def drained(distance, carry):
            other = lax.rem(k + distance, width)
            first(0, group, other, k).wait_send()

            @pl.when(direct(other))
            def _():
                first(1, group, other, k).wait_send()

            @pl.when(passes_on(other))
            def _():
                over_pair(group, other).wait_send()

            for kind in (0, 1):
                over_tau(kind, group, other, t).wait_send()
                over_core(kind, group, other, t, n).wait_send()
                over_core(kind, group, other, 1 - t, n).wait_send()
            return carry
        lax.fori_loop(1, width, drained, 0)
    for kind in (0, 1):
        own_over_core(kind, n).wait_send()
    for copy in greens() + greens_over_core(n):
        copy.wait_send()


def fused_body(width, integrals, occupied, virtual, pattern):
    own_aux, rows, both = integrals.shape[1:]
    basis = both // 2
    levels = pattern[0]
    bf16, f32 = jnp.bfloat16, jnp.float32
    dma = pltpu.SemaphoreType.DMA
    grid = (2, GROUPS, width)
    anywhere = pl.BlockSpec(memory_space=pl.ANY)
    return pl.pallas_call(
        functools.partial(kernel, width),
        out_shape=jax.ShapeDtypeStruct((own_aux, 6 * own_aux), f32),
        in_specs=[anywhere] * 4,
        out_specs=pl.BlockSpec(memory_space=pltpu.VMEM),
        scratch_shapes=[
            pltpu.VMEM((2 * own_aux, basis, both), bf16),
            pltpu.VMEM((2 * own_aux, basis, basis), bf16),
            pltpu.VMEM((both, both), bf16),
            pltpu.VMEM((both, both), bf16),
            pltpu.VMEM(levels.shape, levels.dtype),
            pltpu.VMEM(levels.shape, levels.dtype),
            pltpu.VMEM((both, both), bf16),
            pltpu.VMEM((basis, both), bf16),
            pltpu.VMEM((basis, basis), bf16),
            pltpu.VMEM((own_aux, basis, both), bf16),
            pltpu.VMEM((own_aux, basis, basis), bf16),
            pltpu.VMEM((2 * own_aux, both, basis), bf16),
            pltpu.VMEM((2 * own_aux, basis, basis), bf16),
            pltpu.VMEM((32 * own_aux, 16 * own_aux), f32),
            pltpu.VMEM((own_aux, 2 * own_aux), f32),
            pltpu.VMEM((own_aux, 2 * own_aux), f32),
            dma((5,)), dma(grid), dma(grid), dma(grid), dma(grid),
            dma((2, GROUPS, 2, width)), dma((2, GROUPS, 2, width)),
            dma((2,)), dma((2,)), dma((5,)), dma((5,)), dma(()), dma(()), dma((GROUPS, width)),
        ],
        compiler_params=pltpu.CompilerParams(
            collective_id=0, has_side_effects=True, vmem_limit_bytes=56 * 2**20
        ),
    )(integrals, occupied, virtual, levels)


def body(sizes, integrals, occupied, virtual, pattern):
    if sizes["tau"] == 2 and sizes["narrow"] == 2 and integrals.shape[2] % 16 == 0 and sizes["wide"] % 2 == 0:
        return fused_body(sizes["wide"], integrals, occupied, virtual, pattern)
    return plain_body(integrals, occupied, virtual, pattern)


def solution(mesh):
    in_specs = (
        P(None, "narrow", "wide", None),
        P(("tau", "wide"), None),
        P(("tau", "wide"), None),
        P("wide", None, None),
    )
    out_specs = P(("tau", "wide", "narrow"), None)
    return jax.shard_map(
        functools.partial(body, dict(mesh.shape)),
        mesh=mesh, in_specs=in_specs, out_specs=out_specs, check_vma=False,
    )
```
